128 devices in a mesh: branch: 4 (over x_hi, core), fsdp: 32 (over x_lo, z, y).
Axes of the slice: x: 4 (x_hi: 2, x_lo: 2; x = x_hi * 2 + x_lo), y: 4, z: 4, core: 2. Of those that a mesh axis runs over, the one named last changes fastest.
Arguments:
- attention_out: bfloat16 [4, 4096, 4096], P('branch', 'fsdp'), may hold values from -0.09375 to 0.09375
- tokens: bfloat16 [1024, 4096], P('fsdp', 'branch'), may hold values from -6 to 6
- out_grads: bfloat16 [1024, 4096], P('fsdp', 'branch'), may hold values from -6 to 6
- route_ids: int32 [1024, 2], P('fsdp'), may hold values from 0 to 3, all different within a row; in each aligned block of 32 rows (0 to 31, 32 to 63, ...) at most 18 rows name the same one
- route_gates: float32 [1024, 2], P('fsdp'), may hold values from 0.2 to 1
- gate_weight: bfloat16 [4, 4096, 11008], P('branch', 'fsdp'), may hold values from -0.09375 to 0.09375
- up_weight: bfloat16 [4, 4096, 11008], P('branch', 'fsdp'), may hold values from -0.09375 to 0.09375
- down_weight: bfloat16 [4, 4096, 11008], P('branch', 'fsdp'), may hold values from -0.0546875 to 0.0546875
Outputs:
- merged_attention: bfloat16 [4096, 4096], P('fsdp', 'branch')
- mixed_out: bfloat16 [1024, 4096], P('fsdp', 'branch')
- token_grads: bfloat16 [1024, 4096], P('fsdp', 'branch')
- gate_grads: bfloat16 [4, 4096, 11008], P('branch', None, 'fsdp')
- up_grads: bfloat16 [4, 4096, 11008], P('branch', None, 'fsdp')
- down_grads: bfloat16 [4, 4096, 11008], P('branch', None, 'fsdp')
The draws below stay inside these ranges and needn't reach their ends.
Inputs may be any that keep to these rules, and one draw needn't show every extreme that they name: `route_ids`: each row names two different experts; within each aligned block of 32 rows no expert is named by more than 18 rows, a bound that some block reaches.
All inputs are finite; a program needn't handle non-finite values.
Results may differ from the reference program's by a relative error of at most 0.013.
Values may be sent and summed in bfloat16 or wider, within the bound.
No kernel may reach another device: no remote copies, remote signals or barrier semaphores. Data moves between devices by JAX's collectives and lax.ppermute only.
A program may use at most 192 MiB of HBM per device.

```python
import math
import jax
import jax.numpy as jnp
import numpy as np
from jax import lax

D = 4096
FF = 11008
TOK_DEV = 32
CAP = 18
EXPERTS = 4
TOKENS = 1024
N_BRANCH = 4


def shard_levels(key, shape, split, least, high):
    def one(dim, shards_of):
        heights = jax.random.uniform(jax.random.fold_in(jax.random.fold_in(key, 6), dim), (shards_of,), jnp.float32, least / len(split), high / len(split))
        return jnp.repeat(jnp.exp(heights), shape[dim] // shards_of).reshape((-1,) + (1,) * (len(shape) - dim - 1))

    level = one(*split[0])
    for cut in split[1:]:
        level = level * one(*cut)
    return level


def routed_block(stream_key, own, number, rows, count, top, most, skew):
    ranking = jax.random.permutation(stream_key, count)
    crowded, usual = portions_of(count, rows * top, most, skew, True), portions_of(count, rows * top, most, skew, False)
    places = jnp.arange(count)

    def named(sizes, offset_by):
        used = int((sizes > 0).sum())
        fixed = max(1, used // 4)
        passed = fixed + (places - fixed + offset_by * (used - fixed)) % max(1, count - fixed)
        return jnp.zeros((count,), jnp.int32).at[ranking[jnp.where(places < fixed, places, passed)]].set(jnp.asarray(sizes, jnp.int32))

    sizes = jnp.where(number % 4 == 0, named(crowded, number // 4), named(usual, number - number // 4 - 1))
    mixed = jax.random.permutation(jax.random.fold_in(own, 3), count)
    giver, sink = mixed[0:count // 2 * 2:2], mixed[1:count // 2 * 2:2]
    slack = jnp.minimum(sizes[giver] - 1, most - sizes[sink]) // 2
    slack = jnp.where((giver == ranking[0]) | (sink == ranking[0]) | (sizes[sink] == 0), 0, jnp.maximum(slack, 0))
    passed = jax.random.randint(jax.random.fold_in(own, 4), (count // 2,), 0, 1 << 20) % (slack + 1)
    sizes = sizes.at[giver].add(-passed).at[sink].add(passed)
    labels = jnp.searchsorted(jnp.cumsum(sizes), jnp.arange(rows * top), side="right").astype(jnp.int32)
    listing = labels.reshape(top, rows).T
    listing = listing[jax.random.permutation(jax.random.fold_in(own, 1), rows)]
    offset_by = jax.random.randint(jax.random.fold_in(own, 2), (rows, 1), 0, top)
    return jnp.take_along_axis(listing, (jnp.arange(top)[None, :] + offset_by) % top, axis=1)


def portions_of(number_of, total, most, lean, full):
    portions = [(1 << 20) // math.isqrt(rank ** lean) + 1 for rank in range(1, number_of + 1)]
    largest = most if full else min(most, max(-(-total // number_of), total * portions[0] // sum(portions)))
    least = 1 if total - largest >= number_of - 1 else 0
    given, spare = [largest] + [least] * (number_of - 1), total - largest - least * (number_of - 1)
    while spare > 0:
        movable = [i for i in range(1, number_of) if given[i] < largest] or [i for i in range(1, number_of) if given[i] < most]
        whole, remaining = sum([portions[i] for i in movable]), spare
        for i in movable:
            extra = min(most - given[i], max(1, remaining * portions[i] // whole), spare)
            given[i] = given[i] + extra
            spare = spare - extra
    return np.array(given)


def gaussian(rng, dims, spread, reach, split=(), dtype=jnp.bfloat16):
    entries = spread * jax.random.normal(rng, dims, jnp.float32)
    if split:
        entries = entries * shard_levels(rng, dims, split, -0.22, 0.18)
    return jnp.clip(entries, -reach, reach).astype(dtype)


def setup_inputs(seed: int = 0) -> dict:
    streams_of = jax.random.split(jax.random.key(seed), 9)
    attention_out = gaussian(streams_of[0], (EXPERTS, D, D), D ** -0.5, 0.09375, ((0, 4), (1, 32)))
    tokens = gaussian(streams_of[1], (TOKENS, D), 1.0, 6.0, ((0, 32), (1, 4)))
    out_grads = gaussian(streams_of[2], (TOKENS, D), 1.0, 6.0, ((0, 32), (1, 4)))
    route_ids_keys = jax.random.split(jax.random.fold_in(streams_of[3], 1), TOKENS // TOK_DEV)
    route_ids_turns = jax.random.permutation(jax.random.fold_in(streams_of[3], 3), TOKENS // TOK_DEV)
    route_ids = jax.vmap(lambda own, number: routed_block(jax.random.fold_in(streams_of[3], 2), own, number, TOK_DEV, EXPERTS, 2, CAP, 2))(route_ids_keys, route_ids_turns).reshape((TOKENS, 2))
    route_gates = jnp.clip(0.2 + 0.8 * jax.random.uniform(streams_of[4], (TOKENS, 2), jnp.float32) ** shard_levels(streams_of[4], (TOKENS, 2), ((0, 32),), -0.2, 0.2), 0.2, 1.0)
    gate_weight = gaussian(streams_of[5], (EXPERTS, D, FF), D ** -0.5, 0.09375, ((0, 4), (1, 32)))
    up_weight = gaussian(streams_of[6], (EXPERTS, D, FF), D ** -0.5, 0.09375, ((0, 4), (1, 32)))
    down_weight = gaussian(streams_of[7], (EXPERTS, D, FF), FF ** -0.5, 0.0546875, ((0, 4), (1, 32)))
    return dict(attention_out=attention_out, tokens=tokens, out_grads=out_grads, route_ids=route_ids, route_gates=route_gates, gate_weight=gate_weight, up_weight=up_weight, down_weight=down_weight)


def slot_tables(route_ids, route_gates, experts, capacity):
    expert_ids = lax.broadcasted_iota(jnp.int32, (experts, 1, 1), 0)
    matched = route_ids[None, :, :] == expert_ids
    chosen = jnp.any(matched, axis=2).astype(jnp.int32)
    token_gate = jnp.sum(jnp.where(matched, route_gates[None, :, :], jnp.float32(0.0)), axis=2)
    position = jnp.cumsum(chosen, axis=1) - chosen
    slot_ids = lax.broadcasted_iota(jnp.int32, (1, capacity, 1), 1)
    selector = ((position[:, None, :] == slot_ids) & (chosen[:, None, :] == 1)).astype(jnp.float32)
    slot_gate = jnp.sum(selector * token_gate[:, None, :], axis=2)
    return selector, slot_gate


def reference(attention_out, tokens, out_grads, route_ids, route_gates, gate_weight, up_weight, down_weight):
    highest = lax.Precision.HIGHEST
    merged = (jnp.sum(attention_out.astype(jnp.float32), axis=0) / N_BRANCH).astype(jnp.bfloat16)
    blocks = TOKENS // TOK_DEV
    block_ids = route_ids.reshape(blocks, TOK_DEV, 2)
    block_gates = route_gates.reshape(blocks, TOK_DEV, 2)
    selector, slot_gate = jax.vmap(lambda ids, gates: slot_tables(ids, gates, EXPERTS, CAP))(block_ids, block_gates)
    token_blocks = tokens.reshape(blocks, TOK_DEV, D).astype(jnp.float32)
    grad_blocks = out_grads.reshape(blocks, TOK_DEV, D).astype(jnp.float32)
    mixed = jnp.zeros((blocks, TOK_DEV, D), jnp.float32)
    back = jnp.zeros((blocks, TOK_DEV, D), jnp.float32)
    gate_list, up_list, down_list = [], [], []
    contract_last = (((1,), (1,)), ((), ()))
    contract_first = (((0,), (0,)), ((), ()))
    for expert in range(EXPERTS):
        picker = selector[:, expert]
        weighted = picker * slot_gate[:, expert][:, :, None]
        rows_in = jnp.einsum("jct,jtd->jcd", picker, token_blocks, precision=highest).astype(jnp.bfloat16).reshape(blocks * CAP, D)
        gate_pre = jnp.dot(rows_in, gate_weight[expert], preferred_element_type=jnp.float32)
        up_pre = jnp.dot(rows_in, up_weight[expert], preferred_element_type=jnp.float32)
        sigmoid = jax.nn.sigmoid(gate_pre)
        activated = gate_pre * sigmoid
        hidden = (activated * up_pre).astype(jnp.bfloat16)
        partial_value = lax.dot_general(hidden, down_weight[expert], contract_last, preferred_element_type=jnp.float32)
        mixed = mixed + jnp.einsum("jct,jcd->jtd", weighted, partial_value.reshape(blocks, CAP, D), precision=highest)
        slot_grads = jnp.einsum("jct,jtd->jcd", weighted, grad_blocks, precision=highest).astype(jnp.bfloat16).reshape(blocks * CAP, D)
        hidden_grad = jnp.dot(slot_grads, down_weight[expert], preferred_element_type=jnp.float32)
        down_list.append(lax.dot_general(slot_grads, hidden, contract_first, preferred_element_type=jnp.float32).astype(jnp.bfloat16))
        gate_delta = (hidden_grad * up_pre * sigmoid * (1.0 + gate_pre * (1.0 - sigmoid))).astype(jnp.bfloat16)
        up_delta = (hidden_grad * activated).astype(jnp.bfloat16)
        gate_list.append(lax.dot_general(rows_in, gate_delta, contract_first, preferred_element_type=jnp.float32).astype(jnp.bfloat16))
        up_list.append(lax.dot_general(rows_in, up_delta, contract_first, preferred_element_type=jnp.float32).astype(jnp.bfloat16))
        input_part = lax.dot_general(gate_delta, gate_weight[expert], contract_last, preferred_element_type=jnp.float32)
        input_part = input_part + lax.dot_general(up_delta, up_weight[expert], contract_last, preferred_element_type=jnp.float32)
        back = back + jnp.einsum("jct,jcd->jtd", picker, input_part.reshape(blocks, CAP, D), precision=highest)
    mixed_out = mixed.reshape(TOKENS, D).astype(jnp.bfloat16)
    token_grads = back.reshape(TOKENS, D).astype(jnp.bfloat16)
    return (merged, mixed_out, token_grads, jnp.stack(gate_list), jnp.stack(up_list), jnp.stack(down_list))
```

```python
import jax
import jax.numpy as jnp
from jax import lax
from jax.experimental import pallas as pl
from jax.experimental.pallas import tpu as pltpu
from jax.sharding import Mesh
from jax.sharding import PartitionSpec as P

CAP = 18
BLK = 32
GROUPS = 4
BF = jnp.bfloat16
F32 = jnp.float32
BRANCH = ("xh", "c")
FSDP = ("xl", "z", "y")
PLANE = ("xh", "xl", "z", "y")
CONTRACT_LAST = (((1,), (1,)), ((), ()))
CONTRACT_FIRST = (((0,), (0,)), ((), ()))
VMEM = 44 * 2**20


def call(kernel, prefetch, grid, ins, outs, shapes, name, scratch=()):
    return pl.pallas_call(
        kernel,
        grid_spec=pltpu.PrefetchScalarGridSpec(
            num_scalar_prefetch=prefetch,
            grid=grid,
            in_specs=ins,
            out_specs=outs,
            scratch_shapes=scratch,
        ),
        out_shape=shapes,
        compiler_params=pltpu.CompilerParams(vmem_limit_bytes=VMEM),
        cost_estimate=pl.CostEstimate(flops=1, bytes_accessed=1, transcendentals=0),
        name=name,
    )


def transpose_kernel(w_ref, o_ref):
    o_ref[...] = w_ref[0].T


def transposed(w):
    depth, width = w.shape[1:]
    step = width // 2
    blocks = call(
        transpose_kernel,
        0,
        (2,),
        [pl.BlockSpec((1, depth, step), lambda i: (0, 0, i))],
        pl.BlockSpec((step, depth), lambda i: (i, 0)),
        jax.ShapeDtypeStruct((width, depth), BF),
        "transpose_weight",
    )(w)
    return blocks.reshape(BLK, width // BLK, depth)


def to_owners(blocks):
    return lax.all_to_all(blocks, FSDP, 0, 0, tiled=True)


def wide(ref, first, count):
    return jnp.concatenate([ref[first + j] for j in range(count)], axis=1)


def pick_kernel(sel_ref, gate_ref, x_ref, o_ref):
    factor = jnp.where(pl.program_id(1) == 1, gate_ref[...], F32(1.0))
    slots = sel_ref.shape[1]
    for g in range(GROUPS):
        at = pl.ds(g * slots, slots)
        rows = jnp.dot(sel_ref[g], x_ref[0, g], preferred_element_type=F32)
        o_ref[0, 0, at, :] = (rows * factor[g * slots : (g + 1) * slots]).astype(BF)


def picked_rows(selector, slot_gate, gathered):
    _, slots, per = selector.shape
    width = gathered.shape[3] // 128 // 2 * 128
    total = GROUPS * slots
    return call(
        pick_kernel,
        0,
        (2, 2),
        [
            pl.BlockSpec((GROUPS, slots, per), lambda x, k: (0, 0, 0)),
            pl.BlockSpec((total, 1), lambda x, k: (0, 0)),
            pl.BlockSpec((1, GROUPS, per, width), lambda x, k: (x, 0, 0, k)),
        ],
        pl.BlockSpec((1, 1, total, width), lambda x, k: (k, x, 0, 0)),
        jax.ShapeDtypeStruct((2, 2, total, width), BF),
        "pick_rows",
    )(selector, slot_gate, gathered)


def spread_tokens(spread_ref, values, o_ref):
    slots, per = spread_ref.shape[2], spread_ref.shape[1]
    for g in range(GROUPS):
        part = values[g * slots : (g + 1) * slots]
        rows = jnp.dot(spread_ref[g], part, preferred_element_type=F32)
        o_ref[pl.ds(g * per, per), :] = rows.astype(BF)


def accumulate(half, first, mine_ref, theirs_ref, weight_ref, acc_ref):
    cols = wide(weight_ref, 0, weight_ref.shape[0])
    rows = jnp.where(half == 0, mine_ref[0, 0], theirs_ref[0, 0])
    part = lax.dot_general(rows, cols, CONTRACT_LAST, preferred_element_type=F32)

    @pl.when(first)
    def _():
        acc_ref[...] = part

    @pl.when(jnp.logical_not(first))
    def _():
        acc_ref[...] += part


def expert_kernel(
    core_ref, mine_in, theirs_in, mine_grad, theirs_grad, gate_cols, up_cols, down_cols,
    slot_gate, spread, hidden, gate_delta, up_delta, tokens, gate_acc, up_acc, grad_acc,
):
    half, x = pl.program_id(0), pl.program_id(1)
    first = (half == 0) & (x == 0)
    accumulate(half, first, mine_in, theirs_in, gate_cols, gate_acc)
    accumulate(half, first, mine_in, theirs_in, up_cols, up_acc)
    accumulate(half, first, mine_grad, theirs_grad, down_cols, grad_acc)

    @pl.when((half == 1) & (x == 1))
    def _():
        gate_pre, up_pre, hidden_grad = gate_acc[...], up_acc[...], grad_acc[...]
        sigmoid = jax.nn.sigmoid(gate_pre)
        activated = gate_pre * sigmoid
        product = activated * up_pre
        slope = up_pre * sigmoid * (1.0 + gate_pre * (1.0 - sigmoid))
        hidden[...] = product.astype(BF)
        gate_delta[...] = (hidden_grad * slope).astype(BF)
        up_delta[...] = (hidden_grad * activated).astype(BF)
        spread_tokens(spread, (product * slot_gate[...]).astype(BF), tokens.at[0])
        spread_tokens(spread, gate_delta[...], tokens.at[1])
        spread_tokens(spread, up_delta[...], tokens.at[2])


def row_specs(which, total, width):
    return [
        pl.BlockSpec((1, 1, total, width), lambda h, x, c: (which, jnp.where(h == 0, x, 1), 0, 0)),
        pl.BlockSpec((1, 1, total, width), lambda h, x, c: (which, jnp.where(h == 0, 0, x), 0, 0)),
    ]


def whole(shape):
    return pl.BlockSpec(shape, lambda *_: (0,) * len(shape))


def expert(core, mine, theirs, gate_cols, up_cols, down_cols, slot_gate, spread):
    total, width = mine.shape[2:]
    blocks, units, depth = gate_cols.shape
    tokens = spread.shape[0] * spread.shape[1]
    cols = pl.BlockSpec(
        (blocks // 4, units, depth), lambda h, x, c: (2 * x + jnp.where(h == 0, c[0], 1 - c[0]), 0, 0)
    )
    return call(
        expert_kernel,
        1,
        (2, 2),
        row_specs(0, total, width)
        + row_specs(1, total, width)
        + [cols] * 3
        + [whole(slot_gate.shape), whole(spread.shape)],
        [whole((total, units))] * 3 + [whole((3, tokens, units))],
        [jax.ShapeDtypeStruct((total, units), BF)] * 3
        + [jax.ShapeDtypeStruct((3, tokens, units), BF)],
        "expert",
        scratch=[pltpu.VMEM((total, units), F32)] * 3,
    )(core, mine, theirs, mine, theirs, gate_cols, up_cols, down_cols, slot_gate, spread)


def weight_grad_kernel(core_ref, mine, theirs, *refs):
    count = len(refs) // 2
    rows = jnp.where(pl.program_id(0) == 0, mine[0, 0], theirs[0, 0])
    for delta, out in zip(refs[:count], refs[count:]):
        grad = lax.dot_general(rows, delta[...], CONTRACT_FIRST, preferred_element_type=F32)
        out[...] = grad.astype(BF)


def weight_grads(core, mine, theirs, which, deltas):
    total, width = mine.shape[2:]
    units = deltas[0].shape[1]
    rows = row_specs(which, total, width)
    out = pl.BlockSpec(
        (width, units), lambda h, x, c: (2 * x + jnp.where(h == 0, c[0], 1 - c[0]), 0)
    )
    return call(
        weight_grad_kernel,
        1,
        (2, 2),
        rows + [whole(d.shape) for d in deltas],
        [out] * len(deltas),
        [jax.ShapeDtypeStruct((4 * width, units), BF)] * len(deltas),
        "weight_grads",
    )(core, mine, theirs, *deltas)


def partial_kernel(terms, half_ref, *refs):
    o_ref = refs[-1]
    step = 2
    for first in range(0, refs[1].shape[0], step):
        total = None
        for i in range(terms):
            part = jnp.dot(
                refs[2 * i][...], wide(refs[2 * i + 1], first, step), preferred_element_type=F32
            )
            total = part if total is None else total + part
        at = pl.ds(first * refs[1].shape[2], step * refs[1].shape[2])
        o_ref[0, :, at] = total.astype(BF)


def token_partial(terms, half):
    _, tokens, units = terms[0][0].shape
    blocks, _, depth = terms[0][2].shape
    per = blocks // 8
    quarter = 2 * per * depth
    specs, args = [], []
    for rows, i, weight in terms:
        specs.append(pl.BlockSpec((None, tokens, units), lambda x, n, h, i=i: (i, 0, 0)))
        if weight.shape[0] == blocks:
            index = lambda x, n, h: (4 * x + 2 * h[0] + n, 0, 0)
        else:
            index = lambda x, n, h: (2 * x + n, 0, 0)
        specs.append(pl.BlockSpec((per, units, depth), index))
        args += [rows, weight]
    return call(
        lambda *refs: partial_kernel(len(terms), *refs),
        1,
        (2, 2),
        specs,
        pl.BlockSpec((1, tokens, per * depth), lambda x, n, h: (x, 0, n)),
        jax.ShapeDtypeStruct((2, tokens, quarter), BF),
        "token_partial",
    )(half, *args)


def over_core(x):
    return lax.ppermute(x, "c", [(0, 1), (1, 0)])


def half_blocks(cols, half):
    blocks, units, depth = cols.shape
    cut = cols.reshape(2, 2, blocks // 4, units, depth)
    picked = lax.dynamic_index_in_dim(cut, half, 1, keepdims=False)
    return picked.reshape(blocks // 2, units, depth)


def scattered(mine):
    rows, quarter = mine.shape[1] // BLK, mine.shape[2]
    return lax.all_to_all(mine.reshape(2 * BLK, rows, quarter), PLANE, 0, 0, tiled=True)


def summed(parts):
    return jnp.sum(parts.astype(F32), axis=0).astype(BF)


def route_columns(ids, gates):
    columns, rest = [ids.astype(F32)], gates
    for _ in range(3):
        piece = lax.reduce_precision(rest, 8, 7)
        columns.append(piece)
        rest = rest - piece
    columns = jnp.concatenate(columns, axis=1)
    return jnp.pad(columns, ((0, 0), (0, 128 - columns.shape[1]))).astype(BF)


def routes(columns):
    columns = columns.reshape(-1, columns.shape[-1])[:, :8].astype(F32)
    gates = columns[:, 2:4] + columns[:, 4:6] + columns[:, 6:8]
    return columns[:, :2].astype(jnp.int32), gates


def slot_tables(ids, gates, expert):
    matched = ids == expert
    chosen = jnp.any(matched, axis=-1)
    gate = jnp.sum(jnp.where(matched, gates, F32(0.0)), axis=-1)
    counted = chosen.reshape(BLK, -1).astype(jnp.int32)
    position = jnp.cumsum(counted, axis=1) - counted
    per_group = BLK // GROUPS
    slots = per_group * CAP
    base = (lax.broadcasted_iota(jnp.int32, position.shape, 0) % per_group) * CAP
    slot = jnp.where(counted == 1, base + position, -1).reshape(GROUPS, -1)
    shape = (GROUPS, slots, slot.shape[1])
    selector = lax.broadcasted_iota(jnp.int32, shape, 1) == slot[:, None, :]
    slot_gate = jnp.sum(jnp.where(selector, gate.reshape(GROUPS, 1, -1), F32(0.0)), axis=2)
    spread = lax.broadcasted_iota(jnp.int32, (GROUPS, slot.shape[1], slots), 2) == slot[:, :, None]
    return selector.astype(BF), spread.astype(BF), slot_gate.reshape(-1, 1)


def average(attention):
    me = lax.axis_index(BRANCH)
    share = attention.shape[1] // 4

    def quarter(i):
        return lax.dynamic_slice_in_dim(attention, i * share, share, 1)

    total = quarter(me).astype(F32)
    for shift in range(1, 4):
        sent = quarter((me + shift) % 4)
        there = [(i, (i + shift) % 4) for i in range(4)]
        total = total + lax.ppermute(sent, BRANCH, there).astype(F32)
    return (total / 4).astype(BF)


def together(*arrays):
    return lax.optimization_barrier(arrays)


def on_device(
    attention_out, tokens, out_grads, route_ids, route_gates, gate_weight, up_weight, down_weight
):
    core = lax.axis_index("c")
    expert_id = 2 * lax.axis_index("xh") + core
    sibling = 2 * lax.axis_index("xh") + 1 - core
    core_id = core.reshape(1).astype(jnp.int32)

    width = tokens.shape[1]
    both = jnp.concatenate([tokens, out_grads, route_columns(route_ids, route_gates)], axis=1)
    gathered = lax.all_gather(both, PLANE, axis=0, tiled=True)
    gathered = gathered.reshape(2, GROUPS, -1, both.shape[1])

    gate_blocks = transposed(gate_weight)
    up_blocks, down_blocks = transposed(up_weight), transposed(down_weight)
    gate_cols = to_owners(gate_blocks)
    gate_cols, up_blocks, down_blocks = together(gate_cols, up_blocks, down_blocks)
    up_cols = to_owners(up_blocks)
    up_cols, down_blocks = together(up_cols, down_blocks)
    down_cols = to_owners(down_blocks)
    their_gate = over_core(half_blocks(gate_cols, 1 - core))
    their_up = over_core(half_blocks(up_cols, 1 - core))
    down_cols, gathered = together(down_cols, gathered)

    ids, gates = routes(gathered[0, :, :, 2 * width :])
    selector, spread, slot_gate = slot_tables(ids, gates, expert_id)
    other_selector, _, other_gate = slot_tables(ids, gates, sibling)
    theirs = over_core(picked_rows(other_selector, other_gate, gathered))
    their_down = over_core(half_blocks(down_cols, 1 - core))
    mine = picked_rows(selector, slot_gate, gathered)
    attention, mine = together(attention_out[0], mine)
    merged_attention = average(attention)
    hidden, gate_delta, up_delta, by_token = expert(
        core_id, mine, theirs, gate_cols, up_cols, down_cols, slot_gate, spread
    )
    their_token = over_core(by_token)
    total = token_partial([(by_token, 0, down_cols), (their_token, 0, their_down)], core_id)
    total, merged_attention, their_gate, their_up = together(
        total, merged_attention, their_gate, their_up
    )
    out_parts = scattered(total)

    total = token_partial(
        [
            (by_token, 1, gate_cols),
            (by_token, 2, up_cols),
            (their_token, 1, their_gate),
            (their_token, 2, their_up),
        ],
        core_id,
    )
    gate_grads, up_grads = weight_grads(core_id, mine, theirs, 0, [gate_delta, up_delta])
    (down_grads,) = weight_grads(core_id, mine, theirs, 1, [hidden])
    total, gate_grads, up_grads, down_grads = together(total, gate_grads, up_grads, down_grads)
    grad_parts = scattered(total)
    mixed_out = summed(out_parts)
    grad_parts, mixed_out = together(grad_parts, mixed_out)
    token_grads = summed(grad_parts)
    return (
        merged_attention,
        mixed_out,
        token_grads,
        gate_grads[None],
        up_grads[None],
        down_grads[None],
    )


def solution(mesh):
    fine = Mesh(mesh.devices.reshape(2, 2, 2, 4, 4), ("xh", "c", "xl", "z", "y"))
    return jax.shard_map(
        on_device,
        mesh=fine,
        in_specs=(
            P(BRANCH, FSDP, None),
            P(FSDP, BRANCH),
            P(FSDP, BRANCH),
            P(FSDP, None),
            P(FSDP, None),
            P(BRANCH, FSDP, None),
            P(BRANCH, FSDP, None),
            P(BRANCH, FSDP, None),
        ),
        out_specs=(
            P(FSDP, BRANCH),
            P(FSDP, BRANCH),
            P(FSDP, BRANCH),
            P(BRANCH, None, FSDP),
            P(BRANCH, None, FSDP),
            P(BRANCH, None, FSDP),
        ),
        check_vma=False,
    )
```

```python
import functools
import itertools

import jax
import jax.numpy as jnp
from jax import lax
from jax.experimental import pallas as pl
from jax.experimental.pallas import tpu as pltpu
from jax.sharding import Mesh
from jax.sharding import PartitionSpec as P

CAP = 18
BLK = 32
GROUPS = 4
BF = jnp.bfloat16
F32 = jnp.float32
BRANCH = ("xh", "c")
FSDP = ("xl", "z", "y")
PLANE = ("xh", "xl", "z", "y")
CONTRACT_LAST = (((1,), (1,)), ((), ()))
CONTRACT_FIRST = (((0,), (0,)), ((), ()))
VMEM = 56 * 2**20
RING = 4
AXES = "xzy"
PARTS = ((0, 512, "xzy"), (512, 1024, "zyx"))


def call(kernel, prefetch, grid, ins, outs, shapes, name, scratch=()):
    return pl.pallas_call(
        kernel,
        grid_spec=pltpu.PrefetchScalarGridSpec(
            num_scalar_prefetch=prefetch,
            grid=grid,
            in_specs=ins,
            out_specs=outs,
            scratch_shapes=scratch,
        ),
        out_shape=shapes,
        compiler_params=pltpu.CompilerParams(vmem_limit_bytes=VMEM),
        cost_estimate=pl.CostEstimate(flops=1, bytes_accessed=1, transcendentals=0),
        name=name,
    )


def transpose_kernel(w_ref, o_ref):
    o_ref[...] = w_ref[0].T


def transposed(w):
    depth, width = w.shape[1:]
    step = width // 2
    blocks = call(
        transpose_kernel,
        0,
        (2,),
        [pl.BlockSpec((1, depth, step), lambda i: (0, 0, i))],
        pl.BlockSpec((step, depth), lambda i: (i, 0)),
        jax.ShapeDtypeStruct((width, depth), BF),
        "transpose_weight",
    )(w)
    return blocks.reshape(BLK, width // BLK, depth)


def to_owners(blocks):
    return lax.all_to_all(blocks, FSDP, 0, 0, tiled=True)


def wide(ref, first, count):
    return jnp.concatenate([ref[first + j] for j in range(count)], axis=1)


def pick_kernel(sel_ref, gate_ref, x_ref, o_ref):
    factor = jnp.where(pl.program_id(1) == 1, gate_ref[...], F32(1.0))
    slots = sel_ref.shape[1]
    for g in range(GROUPS):
        at = pl.ds(g * slots, slots)
        rows = jnp.dot(sel_ref[g], x_ref[0, g], preferred_element_type=F32)
        o_ref[0, 0, at, :] = (rows * factor[g * slots : (g + 1) * slots]).astype(BF)


def picked_rows(selector, slot_gate, gathered):
    _, slots, per = selector.shape
    width = gathered.shape[3] // 128 // 2 * 128
    total = GROUPS * slots
    return call(
        pick_kernel,
        0,
        (2, 2),
        [
            pl.BlockSpec((GROUPS, slots, per), lambda x, k: (0, 0, 0)),
            pl.BlockSpec((total, 1), lambda x, k: (0, 0)),
            pl.BlockSpec((1, GROUPS, per, width), lambda x, k: (x, 0, 0, k)),
        ],
        pl.BlockSpec((1, 1, total, width), lambda x, k: (k, x, 0, 0)),
        jax.ShapeDtypeStruct((2, 2, total, width), BF),
        "pick_rows",
    )(selector, slot_gate, gathered)


def spread_tokens(spread_ref, values, o_ref):
    slots, per = spread_ref.shape[2], spread_ref.shape[1]
    rest = jnp.zeros((slots, o_ref.shape[1] - values.shape[1]), BF)
    for g in range(GROUPS):
        part = jnp.concatenate([values[g * slots : (g + 1) * slots], rest], axis=1)
        rows = jnp.dot(spread_ref[g], part, preferred_element_type=F32)
        o_ref[pl.ds(g * per, per), :] = rows.astype(BF)


def accumulate(half, first, mine_ref, theirs_ref, weight_ref, acc_ref):
    cols = wide(weight_ref, 0, weight_ref.shape[0])
    rows = jnp.where(half == 0, mine_ref[0, 0], theirs_ref[0, 0])
    part = lax.dot_general(rows, cols, CONTRACT_LAST, preferred_element_type=F32)

    @pl.when(first)
    def _():
        acc_ref[...] = part

    @pl.when(jnp.logical_not(first))
    def _():
        acc_ref[...] += part


def expert_kernel(
    core_ref, mine_in, theirs_in, mine_grad, theirs_grad, gate_cols, up_cols, down_cols,
    slot_gate, spread, hidden, gate_delta, up_delta, tokens, gate_acc, up_acc, grad_acc,
):
    half, x = pl.program_id(0), pl.program_id(1)
    first = (half == 0) & (x == 0)
    accumulate(half, first, mine_in, theirs_in, gate_cols, gate_acc)
    accumulate(half, first, mine_in, theirs_in, up_cols, up_acc)
    accumulate(half, first, mine_grad, theirs_grad, down_cols, grad_acc)

    @pl.when((half == 1) & (x == 1))
    def _():
        gate_pre, up_pre, hidden_grad = gate_acc[...], up_acc[...], grad_acc[...]
        sigmoid = jax.nn.sigmoid(gate_pre)
        activated = gate_pre * sigmoid
        product = activated * up_pre
        slope = up_pre * sigmoid * (1.0 + gate_pre * (1.0 - sigmoid))
        hidden[...] = product.astype(BF)
        gate_delta[...] = (hidden_grad * slope).astype(BF)
        up_delta[...] = (hidden_grad * activated).astype(BF)
        spread_tokens(spread, (product * slot_gate[...]).astype(BF), tokens.at[0])
        spread_tokens(spread, gate_delta[...], tokens.at[1])
        spread_tokens(spread, up_delta[...], tokens.at[2])


def row_specs(which, total, width):
    return [
        pl.BlockSpec((1, 1, total, width), lambda h, x, c: (which, jnp.where(h == 0, x, 1), 0, 0)),
        pl.BlockSpec((1, 1, total, width), lambda h, x, c: (which, jnp.where(h == 0, 0, x), 0, 0)),
    ]


def whole(shape):
    return pl.BlockSpec(shape, lambda *_: (0,) * len(shape))


def expert(core, mine, theirs, gate_cols, up_cols, down_cols, slot_gate, spread):
    total, width = mine.shape[2:]
    blocks, units, depth = gate_cols.shape
    by_token = (3, spread.shape[0] * spread.shape[1], -(-units // 128) * 128)
    cols = pl.BlockSpec(
        (blocks // 4, units, depth), lambda h, x, c: (2 * x + jnp.where(h == 0, c[0], 1 - c[0]), 0, 0)
    )
    return call(
        expert_kernel,
        1,
        (2, 2),
        row_specs(0, total, width)
        + row_specs(1, total, width)
        + [cols] * 3
        + [whole(slot_gate.shape), whole(spread.shape)],
        [whole((total, units))] * 3 + [whole(by_token)],
        [jax.ShapeDtypeStruct((total, units), BF)] * 3
        + [jax.ShapeDtypeStruct(by_token, BF)],
        "expert",
        scratch=[pltpu.VMEM((total, units), F32)] * 3,
    )(core, mine, theirs, mine, theirs, gate_cols, up_cols, down_cols, slot_gate, spread)


def weight_grad_kernel(core_ref, mine, theirs, *refs):
    count = len(refs) // 2
    rows = jnp.where(pl.program_id(0) == 0, mine[0, 0], theirs[0, 0])
    for delta, out in zip(refs[:count], refs[count:]):
        grad = lax.dot_general(delta[...], rows, CONTRACT_FIRST, preferred_element_type=F32)
        out[...] = grad.astype(BF)


def weight_grads(core, mine, theirs, which, deltas):
    total, width = mine.shape[2:]
    units = deltas[0].shape[1]
    rows = row_specs(which, total, width)
    out = pl.BlockSpec(
        (units, width), lambda h, x, c: (0, 2 * x + jnp.where(h == 0, c[0], 1 - c[0]))
    )
    return call(
        weight_grad_kernel,
        1,
        (2, 2),
        rows + [whole(d.shape) for d in deltas],
        [out] * len(deltas),
        [jax.ShapeDtypeStruct((units, 4 * width), BF)] * len(deltas),
        "weight_grads",
    )(core, mine, theirs, *deltas)


def spots(left, axis):
    strides = {name: RING ** (len(left) - 1 - i) for i, name in enumerate(left)}
    others = [name for name in left if name != axis]
    for number, places in enumerate(itertools.product(range(RING), repeat=len(others))):
        yield number, sum(p * strides[o] for p, o in zip(places, others)), strides[axis]


def along(place_ref, axis, shift):
    return lax.rem(place_ref[1 + AXES.index(axis)] + shift, RING)


def cut(left, part, stage, place_ref, load, pieces):
    axis = PARTS[part][2][stage]
    for shift, piece in enumerate(pieces):
        there = along(place_ref, axis, shift)
        for number, base, stride in spots(left, axis):
            load(base + stride * there, piece, number)


def sums_kernel(place_ref, mine, theirs, gate, up, down, their_gate, their_up, their_down, *refs):
    pieces, whole_ref = refs[:-1], refs[-1]
    x, n = pl.program_id(0), pl.program_id(1)
    units, step = gate.shape[1], 2
    outputs = (
        ((0, down, their_down),),
        ((1, gate, their_gate), (2, up, their_up)),
    )
    for first in range(0, gate.shape[0], step):
        at = slice(first * gate.shape[2], (first + step) * gate.shape[2])
        for t, terms in enumerate(outputs):
            total = None
            for i, own, other in terms:
                for rows, weight in ((mine, own), (theirs, other)):
                    part = jnp.dot(
                        rows[i, :, :units], wide(weight, first, step), preferred_element_type=F32
                    )
                    total = part if total is None else total + part
            rows_of = whole_ref.shape[3]
            total = total.reshape(-1, rows_of, total.shape[1]).astype(BF)
            whole_ref[t, n, pl.ds(x * total.shape[0], total.shape[0]), :, at] = total

    @pl.when((x == 1) & (n == 1))
    def _():
        half = whole_ref.shape[4]
        for p, (low, high, _) in enumerate(PARTS):

            def load(spot, piece, number):
                for t in range(2):
                    for m in range(2):
                        lo, hi = max(low, m * half), min(high, (m + 1) * half)
                        if lo < hi:
                            piece[t, number, :, lo - low : hi - low] = whole_ref[
                                t, m, spot, :, lo - m * half : hi - m * half
                            ]

            cut(AXES, p, 0, place_ref, load, pieces[RING * p : RING * (p + 1)])


def piece_shapes(stage, rows):
    spots_left = (RING ** (2 - stage),) if stage < 2 else ()
    return [
        jax.ShapeDtypeStruct((2,) + spots_left + (rows, high - low), BF)
        for low, high, _ in PARTS
        for _ in range(RING)
    ]


def first_pieces(place, mine, theirs, cols, their_cols):
    _, tokens, padded = mine.shape
    blocks, units, depth = cols[0].shape
    per = blocks // 8
    rows = tokens // BLK
    shapes = piece_shapes(0, rows)
    return call(
        sums_kernel,
        1,
        (2, 2),
        [whole(mine.shape)] * 2
        + [pl.BlockSpec((per, units, depth), lambda x, n, c: (4 * x + 2 * c[0] + n, 0, 0))] * 3
        + [pl.BlockSpec((per, units, depth), lambda x, n, c: (2 * x + n, 0, 0))] * 3,
        [whole(shape.shape) for shape in shapes],
        shapes,
        "token_sums",
        scratch=[pltpu.VMEM((2, 2, 2 * BLK, rows, per * depth), BF)],
    )(place, mine, theirs, *cols, *their_cols)


def add_kernel(stage, place_ref, *refs):
    gathered, outs = refs[: RING * len(PARTS)], refs[RING * len(PARTS) :]
    for p, (low, high, order) in enumerate(PARTS):
        group = gathered[RING * p : RING * (p + 1)]

        def summed(*spot):
            return sum(ref[spot].astype(F32) for ref in group).astype(BF)

        if stage == 3:
            for t in range(2):
                outs[t][:, low:high] = summed(t)
            continue
        left = [name for name in AXES if name not in order[:stage]]

        def load(spot, piece, number):
            for t in range(2):
                if stage == 1:
                    piece[t, number] = summed(t, spot)
                else:
                    piece[t] = summed(t, spot)

        cut(left, p, stage, place_ref, load, outs[RING * p : RING * (p + 1)])


def add_pieces(stage, place, gathered):
    rows = gathered[0].shape[-2]
    if stage == 3:
        shapes = [jax.ShapeDtypeStruct((rows, PARTS[-1][1]), BF)] * 2
    else:
        shapes = piece_shapes(stage, rows)
    return call(
        functools.partial(add_kernel, stage),
        1,
        (1,),
        [whole(piece.shape) for piece in gathered],
        [whole(shape.shape) for shape in shapes],
        shapes,
        "add_pieces",
    )(place, *gathered)


def exchanged(stage, pieces):
    got = list(pieces)
    for shift in (1, 3, 2):
        for p, (_, _, order) in enumerate(PARTS):
            names = {"x": ("xh", "xl")}.get(order[stage], order[stage])
            there = [(i, (i + shift) % RING) for i in range(RING)]
            got[RING * p + shift] = lax.ppermute(pieces[RING * p + shift], names, there)
    return got


def over_core(x):
    return lax.ppermute(x, "c", [(0, 1), (1, 0)])


def half_blocks(cols, half):
    blocks, units, depth = cols.shape
    cut = cols.reshape(2, 2, blocks // 4, units, depth)
    picked = lax.dynamic_index_in_dim(cut, half, 1, keepdims=False)
    return picked.reshape(blocks // 2, units, depth)


def route_columns(ids, gates):
    columns, rest = [ids.astype(F32)], gates
    for _ in range(3):
        piece = lax.reduce_precision(rest, 8, 7)
        columns.append(piece)
        rest = rest - piece
    columns = jnp.concatenate(columns, axis=1)
    return jnp.pad(columns, ((0, 0), (0, 128 - columns.shape[1]))).astype(BF)


def routes(columns):
    columns = columns.reshape(-1, columns.shape[-1])[:, :8].astype(F32)
    gates = columns[:, 2:4] + columns[:, 4:6] + columns[:, 6:8]
    return columns[:, :2].astype(jnp.int32), gates


def slot_tables(ids, gates, expert):
    matched = ids == expert
    chosen = jnp.any(matched, axis=-1)
    gate = jnp.sum(jnp.where(matched, gates, F32(0.0)), axis=-1)
    counted = chosen.reshape(BLK, -1).astype(jnp.int32)
    position = jnp.cumsum(counted, axis=1) - counted
    per_group = BLK // GROUPS
    slots = per_group * CAP
    base = (lax.broadcasted_iota(jnp.int32, position.shape, 0) % per_group) * CAP
    slot = jnp.where(counted == 1, base + position, -1).reshape(GROUPS, -1)
    shape = (GROUPS, slots, slot.shape[1])
    selector = lax.broadcasted_iota(jnp.int32, shape, 1) == slot[:, None, :]
    slot_gate = jnp.sum(jnp.where(selector, gate.reshape(GROUPS, 1, -1), F32(0.0)), axis=2)
    spread = lax.broadcasted_iota(jnp.int32, (GROUPS, slot.shape[1], slots), 2) == slot[:, :, None]
    return selector.astype(BF), spread.astype(BF), slot_gate.reshape(-1, 1)


def average(attention):
    me = lax.axis_index(BRANCH)
    share = attention.shape[1] // 4

    def quarter(i):
        return lax.dynamic_slice_in_dim(attention, i * share, share, 1)

    total = quarter(me).astype(F32)
    for shift in range(1, 4):
        sent = quarter((me + shift) % 4)
        there = [(i, (i + shift) % 4) for i in range(4)]
        total = total + lax.ppermute(sent, BRANCH, there).astype(F32)
    return (total / 4).astype(BF)


def together(*arrays):
    return lax.optimization_barrier(arrays)


def on_device(
    attention_out, tokens, out_grads, route_ids, route_gates, gate_weight, up_weight, down_weight
):
    core = lax.axis_index("c")
    expert_id = 2 * lax.axis_index("xh") + core
    sibling = 2 * lax.axis_index("xh") + 1 - core
    core_id = core.reshape(1).astype(jnp.int32)

    width = tokens.shape[1]
    both = jnp.concatenate([tokens, out_grads, route_columns(route_ids, route_gates)], axis=1)
    gathered = lax.all_gather(both, PLANE, axis=0, tiled=True)
    gathered = gathered.reshape(2, GROUPS, -1, both.shape[1])

    gate_blocks = transposed(gate_weight)
    up_blocks, down_blocks = transposed(up_weight), transposed(down_weight)
    gate_cols = to_owners(gate_blocks)
    gate_cols, up_blocks, down_blocks = together(gate_cols, up_blocks, down_blocks)
    their_gate = over_core(half_blocks(gate_cols, 1 - core))
    up_cols = to_owners(up_blocks)
    up_cols, down_blocks = together(up_cols, down_blocks)
    their_up = over_core(half_blocks(up_cols, 1 - core))
    down_cols = to_owners(down_blocks)
    down_cols, gathered, their_gate, their_up = together(
        down_cols, gathered, their_gate, their_up
    )

    ids, gates = routes(gathered[0, :, :, 2 * width :])
    selector, spread, slot_gate = slot_tables(ids, gates, expert_id)
    other_selector, _, other_gate = slot_tables(ids, gates, sibling)
    theirs = over_core(picked_rows(other_selector, other_gate, gathered))
    their_down = over_core(half_blocks(down_cols, 1 - core))
    mine = picked_rows(selector, slot_gate, gathered)
    mine, theirs, their_down = together(mine, theirs, their_down)
    hidden, gate_delta, up_delta, by_token = expert(
        core_id, mine, theirs, gate_cols, up_cols, down_cols, slot_gate, spread
    )
    their_token, attention = together(over_core(by_token), attention_out[0])
    merged_attention = average(attention)
    place = jnp.stack(
        [core, 2 * lax.axis_index("xh") + lax.axis_index("xl"), lax.axis_index("z"), lax.axis_index("y")]
    ).astype(jnp.int32)
    pieces = first_pieces(
        place,
        by_token,
        their_token,
        (gate_cols, up_cols, down_cols),
        (their_gate, their_up, their_down),
    )
    got = exchanged(0, pieces)
    gate_grads, up_grads = weight_grads(core_id, mine, theirs, 0, [gate_delta, up_delta])
    (down_grads,) = weight_grads(core_id, mine, theirs, 1, [hidden])
    *got, gate_grads, up_grads, down_grads = together(*got, gate_grads, up_grads, down_grads)
    got = exchanged(1, add_pieces(1, place, got))
    got = exchanged(2, add_pieces(2, place, got))
    mixed_out, token_grads = add_pieces(3, place, got)
    return (
        merged_attention,
        mixed_out,
        token_grads,
        gate_grads.T[None],
        up_grads.T[None],
        down_grads.T[None],
    )


def solution(mesh):
    fine = Mesh(mesh.devices.reshape(2, 2, 2, 4, 4), ("xh", "c", "xl", "z", "y"))
    return jax.shard_map(
        on_device,
        mesh=fine,
        in_specs=(
            P(BRANCH, FSDP, None),
            P(FSDP, BRANCH),
            P(FSDP, BRANCH),
            P(FSDP, None),
            P(FSDP, None),
            P(BRANCH, FSDP, None),
            P(BRANCH, FSDP, None),
            P(BRANCH, FSDP, None),
        ),
        out_specs=(
            P(FSDP, BRANCH),
            P(FSDP, BRANCH),
            P(FSDP, BRANCH),
            P(BRANCH, None, FSDP),
            P(BRANCH, None, FSDP),
            P(BRANCH, None, FSDP),
        ),
        check_vma=False,
    )
```

```python
import functools
import itertools

import jax
import jax.numpy as jnp
from jax import lax
from jax.experimental import pallas as pl
from jax.experimental.pallas import tpu as pltpu
from jax.sharding import Mesh
from jax.sharding import PartitionSpec as P

CAP = 18
BLK = 32
GROUPS = 4
BF = jnp.bfloat16
F32 = jnp.float32
BRANCH = ("xh", "c")
FSDP = ("xl", "z", "y")
PLANE = ("xh", "xl", "z", "y")
CONTRACT_LAST = (((1,), (1,)), ((), ()))
CONTRACT_FIRST = (((0,), (0,)), ((), ()))
VMEM = 56 * 2**20
RING = 4
AXES = "xzy"
SHIFTS = (0, 1, 3, 2)
PARTS = ((0, 512, "xzy"), (512, 1024, "zyx"))


def call(kernel, prefetch, grid, ins, outs, shapes, name, scratch=()):
    return pl.pallas_call(
        kernel,
        grid_spec=pltpu.PrefetchScalarGridSpec(
            num_scalar_prefetch=prefetch,
            grid=grid,
            in_specs=ins,
            out_specs=outs,
            scratch_shapes=scratch,
        ),
        out_shape=shapes,
        compiler_params=pltpu.CompilerParams(vmem_limit_bytes=VMEM),
        cost_estimate=pl.CostEstimate(flops=1, bytes_accessed=1, transcendentals=0),
        name=name,
    )


def transpose_kernel(w_ref, o_ref):
    o_ref[...] = w_ref[0].T


def transposed(w):
    depth, width = w.shape[1:]
    step = width // 2
    blocks = call(
        transpose_kernel,
        0,
        (2,),
        [pl.BlockSpec((1, depth, step), lambda i: (0, 0, i))],
        pl.BlockSpec((step, depth), lambda i: (i, 0)),
        jax.ShapeDtypeStruct((width, depth), BF),
        "transpose_weight",
    )(w)
    return blocks.reshape(BLK, width // BLK, depth)


def to_owners(blocks):
    return lax.all_to_all(blocks, FSDP, 0, 0, tiled=True)


def wide(ref, first, count):
    return jnp.concatenate([ref[first + j] for j in range(count)], axis=1)


def pick_kernel(sel_ref, gate_ref, x_ref, o_ref):
    factor = jnp.where(pl.program_id(1) == 1, gate_ref[...], F32(1.0))
    slots = sel_ref.shape[1]
    for g in range(GROUPS):
        at = pl.ds(g * slots, slots)
        rows = jnp.dot(sel_ref[g], x_ref[0, g], preferred_element_type=F32)
        o_ref[0, 0, at, :] = (rows * factor[g * slots : (g + 1) * slots]).astype(BF)


def picked_rows(selector, slot_gate, gathered):
    _, slots, per = selector.shape
    width = gathered.shape[3] // 128 // 2 * 128
    total = GROUPS * slots
    return call(
        pick_kernel,
        0,
        (2, 2),
        [
            pl.BlockSpec((GROUPS, slots, per), lambda x, k: (0, 0, 0)),
            pl.BlockSpec((total, 1), lambda x, k: (0, 0)),
            pl.BlockSpec((1, GROUPS, per, width), lambda x, k: (x, 0, 0, k)),
        ],
        pl.BlockSpec((1, 1, total, width), lambda x, k: (k, x, 0, 0)),
        jax.ShapeDtypeStruct((2, 2, total, width), BF),
        "pick_rows",
    )(selector, slot_gate, gathered)


def spread_tokens(spread_ref, values, o_ref):
    slots, per = spread_ref.shape[2], spread_ref.shape[1]
    rest = jnp.zeros((slots, o_ref.shape[1] - values.shape[1]), BF)
    for g in range(GROUPS):
        part = jnp.concatenate([values[g * slots : (g + 1) * slots], rest], axis=1)
        rows = jnp.dot(spread_ref[g], part, preferred_element_type=F32)
        o_ref[pl.ds(g * per, per), :] = rows.astype(BF)


def accumulate(half, first, mine_ref, theirs_ref, weight_ref, acc_ref):
    cols = wide(weight_ref, 0, weight_ref.shape[0])
    rows = jnp.where(half == 0, mine_ref[0, 0], theirs_ref[0, 0])
    part = lax.dot_general(rows, cols, CONTRACT_LAST, preferred_element_type=F32)

    @pl.when(first)
    def _():
        acc_ref[...] = part

    @pl.when(jnp.logical_not(first))
    def _():
        acc_ref[...] += part


def expert_kernel(
    core_ref, mine_in, theirs_in, mine_grad, theirs_grad, gate_cols, up_cols, down_cols,
    slot_gate, spread, hidden, gate_delta, up_delta, tokens, gate_acc, up_acc, grad_acc,
):
    half, x = pl.program_id(0), pl.program_id(1)
    first = (half == 0) & (x == 0)
    accumulate(half, first, mine_in, theirs_in, gate_cols, gate_acc)
    accumulate(half, first, mine_in, theirs_in, up_cols, up_acc)
    accumulate(half, first, mine_grad, theirs_grad, down_cols, grad_acc)

    @pl.when((half == 1) & (x == 1))
    def _():
        gate_pre, up_pre, hidden_grad = gate_acc[...], up_acc[...], grad_acc[...]
        sigmoid = jax.nn.sigmoid(gate_pre)
        activated = gate_pre * sigmoid
        product = activated * up_pre
        slope = up_pre * sigmoid * (1.0 + gate_pre * (1.0 - sigmoid))
        hidden[...] = product.astype(BF)
        gate_delta[...] = (hidden_grad * slope).astype(BF)
        up_delta[...] = (hidden_grad * activated).astype(BF)
        spread_tokens(spread, (product * slot_gate[...]).astype(BF), tokens.at[0])
        spread_tokens(spread, gate_delta[...], tokens.at[1])
        spread_tokens(spread, up_delta[...], tokens.at[2])


def row_specs(which, total, width):
    return [
        pl.BlockSpec((1, 1, total, width), lambda h, x, c: (which, jnp.where(h == 0, x, 1), 0, 0)),
        pl.BlockSpec((1, 1, total, width), lambda h, x, c: (which, jnp.where(h == 0, 0, x), 0, 0)),
    ]


def whole(shape):
    return pl.BlockSpec(shape, lambda *_: (0,) * len(shape))


def expert(core, mine, theirs, gate_cols, up_cols, down_cols, slot_gate, spread):
    total, width = mine.shape[2:]
    blocks, units, depth = gate_cols.shape
    by_token = (3, spread.shape[0] * spread.shape[1], -(-units // 128) * 128)
    cols = pl.BlockSpec(
        (blocks // 4, units, depth), lambda h, x, c: (2 * x + jnp.where(h == 0, c[0], 1 - c[0]), 0, 0)
    )
    return call(
        expert_kernel,
        1,
        (2, 2),
        row_specs(0, total, width)
        + row_specs(1, total, width)
        + [cols] * 3
        + [whole(slot_gate.shape), whole(spread.shape)],
        [whole((total, units))] * 3 + [whole(by_token)],
        [jax.ShapeDtypeStruct((total, units), BF)] * 3
        + [jax.ShapeDtypeStruct(by_token, BF)],
        "expert",
        scratch=[pltpu.VMEM((total, units), F32)] * 3,
    )(core, mine, theirs, mine, theirs, gate_cols, up_cols, down_cols, slot_gate, spread)


def weight_grad_kernel(core_ref, mine, theirs, *refs):
    count = len(refs) // 2
    rows = jnp.where(pl.program_id(0) == 0, mine[0, 0], theirs[0, 0])
    for delta, out in zip(refs[:count], refs[count:]):
        grad = lax.dot_general(delta[...], rows, CONTRACT_FIRST, preferred_element_type=F32)
        out[...] = grad.astype(BF)


def weight_grads(core, mine, theirs, which, deltas):
    total, width = mine.shape[2:]
    units = deltas[0].shape[1]
    rows = row_specs(which, total, width)
    out = pl.BlockSpec(
        (units, width), lambda h, x, c: (0, 2 * x + jnp.where(h == 0, c[0], 1 - c[0]))
    )
    return call(
        weight_grad_kernel,
        1,
        (2, 2),
        rows + [whole(d.shape) for d in deltas],
        [out] * len(deltas),
        [jax.ShapeDtypeStruct((units, 4 * width), BF)] * len(deltas),
        "weight_grads",
    )(core, mine, theirs, *deltas)


def spots(left, axis):
    strides = {name: RING ** (len(left) - 1 - i) for i, name in enumerate(left)}
    others = [name for name in left if name != axis]
    for number, places in enumerate(itertools.product(range(RING), repeat=len(others))):
        yield number, sum(p * strides[o] for p, o in zip(places, others)), strides[axis]


def along(place_ref, axis, shift):
    return lax.rem(place_ref[1 + AXES.index(axis)] + shift, RING)


def by_part(refs):
    return list(refs[:RING]), [refs[RING].at[i] for i in range(RING)]


def cut(left, part, stage, place_ref, load, pieces):
    axis = PARTS[part][2][stage]
    for i, piece in enumerate(pieces):
        there = along(place_ref, axis, SHIFTS[i]) if part == 0 else i
        for number, base, stride in spots(left, axis):
            load(base + stride * there, piece, number)


def sums_kernel(place_ref, mine, theirs, gate, up, down, their_gate, their_up, their_down, *refs):
    pieces, whole_ref = refs[:-1], refs[-1]
    x, n = pl.program_id(0), pl.program_id(1)
    units, step = gate.shape[1], 2
    outputs = (
        ((0, down, their_down),),
        ((1, gate, their_gate), (2, up, their_up)),
    )
    for first in range(0, gate.shape[0], step):
        at = slice(first * gate.shape[2], (first + step) * gate.shape[2])
        for t, terms in enumerate(outputs):
            total = None
            for i, own, other in terms:
                for rows, weight in ((mine, own), (theirs, other)):
                    part = jnp.dot(
                        rows[i, :, :units], wide(weight, first, step), preferred_element_type=F32
                    )
                    total = part if total is None else total + part
            rows_of = whole_ref.shape[3]
            total = total.reshape(-1, rows_of, total.shape[1]).astype(BF)
            whole_ref[t, n, pl.ds(x * total.shape[0], total.shape[0]), :, at] = total

    @pl.when((x == 1) & (n == 1))
    def _():
        half = whole_ref.shape[4]
        for p, (low, high, _) in enumerate(PARTS):

            def load(spot, piece, number):
                for t in range(2):
                    for m in range(2):
                        lo, hi = max(low, m * half), min(high, (m + 1) * half)
                        if lo < hi:
                            piece[t, number, :, lo - low : hi - low] = whole_ref[
                                t, m, spot, :, lo - m * half : hi - m * half
                            ]

            cut(AXES, p, 0, place_ref, load, by_part(pieces)[p])


def piece_shapes(rows):
    lead = (2, RING**2, rows)
    width = [high - low for low, high, _ in PARTS]
    first = jax.ShapeDtypeStruct(lead + (width[0],), BF)
    return [first] * RING + [jax.ShapeDtypeStruct((RING, *lead, width[1]), BF)]


def first_pieces(place, mine, theirs, cols, their_cols):
    _, tokens, padded = mine.shape
    blocks, units, depth = cols[0].shape
    per = blocks // 8
    rows = tokens // BLK
    shapes = piece_shapes(rows)
    return call(
        sums_kernel,
        1,
        (2, 2),
        [whole(mine.shape)] * 2
        + [pl.BlockSpec((per, units, depth), lambda x, n, c: (4 * x + 2 * c[0] + n, 0, 0))] * 3
        + [pl.BlockSpec((per, units, depth), lambda x, n, c: (2 * x + n, 0, 0))] * 3,
        [whole(shape.shape) for shape in shapes],
        shapes,
        "token_sums",
        scratch=[pltpu.VMEM((2, 2, 2 * BLK, rows, per * depth), BF)],
    )(place, mine, theirs, *cols, *their_cols)


def added(pieces):
    return sum(piece.astype(F32) for piece in pieces).astype(BF)


def add_first_kernel(place_ref, *refs):
    pieces, outs = by_part(refs[: RING + 1]), refs[RING + 1 :]

    def load(spot, piece, number):
        piece[0, number] = added([ref[0, spot] for ref in pieces[0]])

    left = [name for name in AXES if name != PARTS[0][2][0]]
    cut(left, 0, 1, place_ref, load, outs[:RING])
    for spot in range(RING**2):
        outs[RING][spot, 0] = added([ref[0, spot] for ref in pieces[1]])


def add_second_kernel(place_ref, *refs):
    pieces, outs = refs[:RING], refs[RING:]

    def load(spot, piece, number):
        piece[0] = added([ref[0, spot] for ref in pieces])

    cut([PARTS[0][2][2]], 0, 2, place_ref, load, outs)


def add_last_kernel(place_ref, *refs):
    pieces, second, out = refs[:RING], refs[RING], refs[RING + 1]
    (low, middle, _), (_, high, _) = PARTS
    out[0, :, low:middle] = added([ref[0] for ref in pieces])
    out[0, :, middle:high] = added([second[i, 0] for i in range(second.shape[0])])


def each_result(kernel, place, arrays, shapes):
    def spec(shape, stacked):
        if stacked:
            return pl.BlockSpec(
                (shape[0], 1, *shape[2:]), lambda t, *_: (0, t) + (0,) * (len(shape) - 2)
            )
        return pl.BlockSpec((1, *shape[1:]), lambda t, *_: (t,) + (0,) * (len(shape) - 1))

    return call(
        kernel,
        1,
        (2,),
        [spec(array.shape, i >= RING) for i, array in enumerate(arrays)],
        [spec(shape.shape, i >= RING) for i, shape in enumerate(shapes)],
        shapes,
        "add_pieces",
    )(place, *arrays)


def axes_of(order):
    return sum(({"x": ("xh", "xl")}.get(name, (name,)) for name in order), ())


def to_shifts(stage, pieces):
    got = [pieces[0]]
    for piece, shift in zip(pieces[1:], SHIFTS[1:]):
        there = [(j, (j + shift) % RING) for j in range(RING)]
        got.append(lax.ppermute(piece, axes_of(PARTS[0][2][stage]), there))
    return got


def reduced(place, pieces):
    rows, width = pieces[0].shape[-2:]
    other = PARTS[1][1] - PARTS[1][0]
    one = jax.ShapeDtypeStruct((2, RING, rows, width), BF)
    many = jax.ShapeDtypeStruct((RING**2, 2, rows, other), BF)
    *first, second = each_result(add_first_kernel, place, pieces, [one] * RING + [many])
    left = "".join(name for name in AXES if name != PARTS[1][2][0])
    second = lax.all_to_all(second, axes_of(left), 0, 0, tiled=True)
    one = jax.ShapeDtypeStruct((2, rows, width), BF)
    first = each_result(add_second_kernel, place, to_shifts(1, first), [one] * RING)
    whole_result = jax.ShapeDtypeStruct((2, rows, PARTS[1][1]), BF)
    (results,) = each_result(
        add_last_kernel, place, to_shifts(2, first) + [second], [whole_result]
    )
    return results


def over_core(x):
    return lax.ppermute(x, "c", [(0, 1), (1, 0)])


def half_blocks(cols, half):
    blocks, units, depth = cols.shape
    cut = cols.reshape(2, 2, blocks // 4, units, depth)
    picked = lax.dynamic_index_in_dim(cut, half, 1, keepdims=False)
    return picked.reshape(blocks // 2, units, depth)


def route_columns(ids, gates):
    columns, rest = [ids.astype(F32)], gates
    for _ in range(3):
        piece = lax.reduce_precision(rest, 8, 7)
        columns.append(piece)
        rest = rest - piece
    columns = jnp.concatenate(columns, axis=1)
    return jnp.pad(columns, ((0, 0), (0, 128 - columns.shape[1]))).astype(BF)


def routes(columns):
    columns = columns.reshape(-1, columns.shape[-1])[:, :8].astype(F32)
    gates = columns[:, 2:4] + columns[:, 4:6] + columns[:, 6:8]
    return columns[:, :2].astype(jnp.int32), gates


def slot_tables(ids, gates, expert):
    matched = ids == expert
    chosen = jnp.any(matched, axis=-1)
    gate = jnp.sum(jnp.where(matched, gates, F32(0.0)), axis=-1)
    counted = chosen.reshape(BLK, -1).astype(jnp.int32)
    position = jnp.cumsum(counted, axis=1) - counted
    per_group = BLK // GROUPS
    slots = per_group * CAP
    base = (lax.broadcasted_iota(jnp.int32, position.shape, 0) % per_group) * CAP
    slot = jnp.where(counted == 1, base + position, -1).reshape(GROUPS, -1)
    shape = (GROUPS, slots, slot.shape[1])
    selector = lax.broadcasted_iota(jnp.int32, shape, 1) == slot[:, None, :]
    slot_gate = jnp.sum(jnp.where(selector, gate.reshape(GROUPS, 1, -1), F32(0.0)), axis=2)
    spread = lax.broadcasted_iota(jnp.int32, (GROUPS, slot.shape[1], slots), 2) == slot[:, :, None]
    return selector.astype(BF), spread.astype(BF), slot_gate.reshape(-1, 1)


def average(attention):
    me = lax.axis_index(BRANCH)
    share = attention.shape[1] // 4

    def quarter(i):
        return lax.dynamic_slice_in_dim(attention, i * share, share, 1)

    total = quarter(me).astype(F32)
    for shift in range(1, 4):
        sent = quarter((me + shift) % 4)
        there = [(i, (i + shift) % 4) for i in range(4)]
        total = total + lax.ppermute(sent, BRANCH, there).astype(F32)
    return (total / 4).astype(BF)


def together(*arrays):
    return lax.optimization_barrier(arrays)


def on_device(
    attention_out, tokens, out_grads, route_ids, route_gates, gate_weight, up_weight, down_weight
):
    core = lax.axis_index("c")
    expert_id = 2 * lax.axis_index("xh") + core
    sibling = 2 * lax.axis_index("xh") + 1 - core
    core_id = core.reshape(1).astype(jnp.int32)

    width = tokens.shape[1]
    both = jnp.concatenate([tokens, out_grads, route_columns(route_ids, route_gates)], axis=1)
    gathered = lax.all_gather(both, PLANE, axis=0, tiled=True)
    gathered = gathered.reshape(2, GROUPS, -1, both.shape[1])

    gate_blocks = transposed(gate_weight)
    up_blocks, down_blocks = transposed(up_weight), transposed(down_weight)
    gate_cols = to_owners(gate_blocks)
    merged_attention = average(attention_out[0])
    gate_cols, up_blocks, down_blocks, merged_attention = together(
        gate_cols, up_blocks, down_blocks, merged_attention
    )
    their_gate = over_core(half_blocks(gate_cols, 1 - core))
    up_cols = to_owners(up_blocks)
    up_cols, down_blocks = together(up_cols, down_blocks)
    their_up = over_core(half_blocks(up_cols, 1 - core))
    down_cols = to_owners(down_blocks)
    down_cols, gathered, their_gate, their_up = together(
        down_cols, gathered, their_gate, their_up
    )

    ids, gates = routes(gathered[0, :, :, 2 * width :])
    selector, spread, slot_gate = slot_tables(ids, gates, expert_id)
    other_selector, _, other_gate = slot_tables(ids, gates, sibling)
    theirs = over_core(picked_rows(other_selector, other_gate, gathered))
    their_down = over_core(half_blocks(down_cols, 1 - core))
    mine = picked_rows(selector, slot_gate, gathered)
    mine, theirs, their_down = together(mine, theirs, their_down)
    hidden, gate_delta, up_delta, by_token = expert(
        core_id, mine, theirs, gate_cols, up_cols, down_cols, slot_gate, spread
    )
    their_token = over_core(by_token)
    place = jnp.stack(
        [core, 2 * lax.axis_index("xh") + lax.axis_index("xl"), lax.axis_index("z"), lax.axis_index("y")]
    ).astype(jnp.int32)
    pieces = first_pieces(
        place,
        by_token,
        their_token,
        (gate_cols, up_cols, down_cols),
        (their_gate, their_up, their_down),
    )
    got = to_shifts(0, pieces[:RING])
    got.append(lax.all_to_all(pieces[RING], axes_of(PARTS[1][2][0]), 0, 0, tiled=True))
    gate_grads, up_grads = weight_grads(core_id, mine, theirs, 0, [gate_delta, up_delta])
    (down_grads,) = weight_grads(core_id, mine, theirs, 1, [hidden])
    *got, gate_grads, up_grads, down_grads = together(*got, gate_grads, up_grads, down_grads)
    results = reduced(place, got)
    mixed_out, token_grads = results[0], results[1]
    return (
        merged_attention,
        mixed_out,
        token_grads,
        gate_grads.T[None],
        up_grads.T[None],
        down_grads.T[None],
    )


def solution(mesh):
    fine = Mesh(mesh.devices.reshape(2, 2, 2, 4, 4), ("xh", "c", "xl", "z", "y"))
    return jax.shard_map(
        on_device,
        mesh=fine,
        in_specs=(
            P(BRANCH, FSDP, None),
            P(FSDP, BRANCH),
            P(FSDP, BRANCH),
            P(FSDP, None),
            P(FSDP, None),
            P(BRANCH, FSDP, None),
            P(BRANCH, FSDP, None),
            P(BRANCH, FSDP, None),
        ),
        out_specs=(
            P(FSDP, BRANCH),
            P(FSDP, BRANCH),
            P(FSDP, BRANCH),
            P(BRANCH, None, FSDP),
            P(BRANCH, None, FSDP),
            P(BRANCH, None, FSDP),
        ),
        check_vma=False,
    )
```

```python
import functools
import itertools

import jax
import jax.numpy as jnp
from jax import lax
from jax.experimental import pallas as pl
from jax.experimental.pallas import tpu as pltpu
from jax.sharding import Mesh
from jax.sharding import PartitionSpec as P

CAP = 18
BLK = 32
GROUPS = 4
BF = jnp.bfloat16
F32 = jnp.float32
BRANCH = ("xh", "c")
FSDP = ("xl", "z", "y")
PLANE = ("xh", "xl", "z", "y")
CONTRACT_LAST = (((1,), (1,)), ((), ()))
CONTRACT_FIRST = (((0,), (0,)), ((), ()))
VMEM = 56 * 2**20
RING = 4
AXES = "xzy"
SHIFTS = (0, 1, 3, 2)
PARTS = ((0, 512, "xzy"), (512, 1024, "zyx"))


def call(kernel, prefetch, grid, ins, outs, shapes, name, scratch=()):
    return pl.pallas_call(
        kernel,
        grid_spec=pltpu.PrefetchScalarGridSpec(
            num_scalar_prefetch=prefetch,
            grid=grid,
            in_specs=ins,
            out_specs=outs,
            scratch_shapes=scratch,
        ),
        out_shape=shapes,
        compiler_params=pltpu.CompilerParams(vmem_limit_bytes=VMEM),
        cost_estimate=pl.CostEstimate(flops=1, bytes_accessed=1, transcendentals=0),
        name=name,
    )


def transpose_kernel(w_ref, o_ref):
    o_ref[...] = w_ref[0].T


def transposed(w):
    depth, width = w.shape[1:]
    step = width // 2
    blocks = call(
        transpose_kernel,
        0,
        (2,),
        [pl.BlockSpec((1, depth, step), lambda i: (0, 0, i))],
        pl.BlockSpec((step, depth), lambda i: (i, 0)),
        jax.ShapeDtypeStruct((width, depth), BF),
        "transpose_weight",
    )(w)
    return blocks.reshape(BLK, width // BLK, depth)


def to_owners(blocks):
    return lax.all_to_all(blocks, FSDP, 0, 0, tiled=True)


def wide(ref, first, count):
    return jnp.concatenate([ref[first + j] for j in range(count)], axis=1)


def pick_kernel(sel_ref, gate_ref, x_ref, o_ref):
    factor = jnp.where(pl.program_id(1) == 1, gate_ref[...], F32(1.0))
    slots = sel_ref.shape[1]
    for g in range(GROUPS):
        at = pl.ds(g * slots, slots)
        rows = jnp.dot(sel_ref[g], x_ref[0, g], preferred_element_type=F32)
        o_ref[0, 0, at, :] = (rows * factor[g * slots : (g + 1) * slots]).astype(BF)


def picked_rows(selector, slot_gate, gathered):
    _, slots, per = selector.shape
    width = gathered.shape[3] // 128 // 2 * 128
    total = GROUPS * slots
    return call(
        pick_kernel,
        0,
        (2, 2),
        [
            pl.BlockSpec((GROUPS, slots, per), lambda x, k: (0, 0, 0)),
            pl.BlockSpec((total, 1), lambda x, k: (0, 0)),
            pl.BlockSpec((1, GROUPS, per, width), lambda x, k: (x, 0, 0, k)),
        ],
        pl.BlockSpec((1, 1, total, width), lambda x, k: (k, x, 0, 0)),
        jax.ShapeDtypeStruct((2, 2, total, width), BF),
        "pick_rows",
    )(selector, slot_gate, gathered)


def spread_tokens(spread_ref, values, o_ref):
    slots, per = spread_ref.shape[2], spread_ref.shape[1]
    rest = jnp.zeros((slots, o_ref.shape[1] - values.shape[1]), BF)
    for g in range(GROUPS):
        part = jnp.concatenate([values[g * slots : (g + 1) * slots], rest], axis=1)
        rows = jnp.dot(spread_ref[g], part, preferred_element_type=F32)
        o_ref[pl.ds(g * per, per), :] = rows.astype(BF)


def accumulate(half, first, mine_ref, theirs_ref, weight_ref, acc_ref):
    cols = wide(weight_ref, 0, weight_ref.shape[0])
    rows = jnp.where(half == 0, mine_ref[0, 0], theirs_ref[0, 0])
    part = lax.dot_general(rows, cols, CONTRACT_LAST, preferred_element_type=F32)

    @pl.when(first)
    def _():
        acc_ref[...] = part

    @pl.when(jnp.logical_not(first))
    def _():
        acc_ref[...] += part


def expert_kernel(
    core_ref, mine_in, theirs_in, mine_grad, theirs_grad, gate_cols, up_cols, down_cols,
    slot_gate, spread, hidden, gate_delta, up_delta, tokens, gate_acc, up_acc, grad_acc,
):
    half, x = pl.program_id(0), pl.program_id(1)
    first = (half == 0) & (x == 0)
    accumulate(half, first, mine_in, theirs_in, gate_cols, gate_acc)
    accumulate(half, first, mine_in, theirs_in, up_cols, up_acc)
    accumulate(half, first, mine_grad, theirs_grad, down_cols, grad_acc)

    @pl.when((half == 1) & (x == 1))
    def _():
        gate_pre, up_pre, hidden_grad = gate_acc[...], up_acc[...], grad_acc[...]
        sigmoid = jax.nn.sigmoid(gate_pre)
        activated = gate_pre * sigmoid
        product = activated * up_pre
        slope = up_pre * sigmoid * (1.0 + gate_pre * (1.0 - sigmoid))
        hidden[...] = product.astype(BF)
        gate_delta[...] = (hidden_grad * slope).astype(BF)
        up_delta[...] = (hidden_grad * activated).astype(BF)
        spread_tokens(spread, (product * slot_gate[...]).astype(BF), tokens.at[0])
        spread_tokens(spread, gate_delta[...], tokens.at[1])
        spread_tokens(spread, up_delta[...], tokens.at[2])


def row_specs(which, total, width):
    return [
        pl.BlockSpec((1, 1, total, width), lambda h, x, c: (which, jnp.where(h == 0, x, 1), 0, 0)),
        pl.BlockSpec((1, 1, total, width), lambda h, x, c: (which, jnp.where(h == 0, 0, x), 0, 0)),
    ]


def whole(shape):
    return pl.BlockSpec(shape, lambda *_: (0,) * len(shape))


def expert(core, mine, theirs, gate_cols, up_cols, down_cols, slot_gate, spread):
    total, width = mine.shape[2:]
    blocks, units, depth = gate_cols.shape
    by_token = (3, spread.shape[0] * spread.shape[1], -(-units // 128) * 128)
    cols = pl.BlockSpec(
        (blocks // 4, units, depth), lambda h, x, c: (2 * x + jnp.where(h == 0, c[0], 1 - c[0]), 0, 0)
    )
    return call(
        expert_kernel,
        1,
        (2, 2),
        row_specs(0, total, width)
        + row_specs(1, total, width)
        + [cols] * 3
        + [whole(slot_gate.shape), whole(spread.shape)],
        [whole((total, units))] * 3 + [whole(by_token)],
        [jax.ShapeDtypeStruct((total, units), BF)] * 3
        + [jax.ShapeDtypeStruct(by_token, BF)],
        "expert",
        scratch=[pltpu.VMEM((total, units), F32)] * 3,
    )(core, mine, theirs, mine, theirs, gate_cols, up_cols, down_cols, slot_gate, spread)


def weight_grad_kernel(core_ref, mine, theirs, *refs):
    count = len(refs) // 2
    rows = jnp.where(pl.program_id(0) == 0, mine[0, 0], theirs[0, 0])
    for delta, out in zip(refs[:count], refs[count:]):
        grad = lax.dot_general(delta[...], rows, CONTRACT_FIRST, preferred_element_type=F32)
        out[...] = grad.astype(BF)


def weight_grads(core, mine, theirs, which, deltas):
    total, width = mine.shape[2:]
    units = deltas[0].shape[1]
    rows = row_specs(which, total, width)
    out = pl.BlockSpec(
        (units, width), lambda h, x, c: (0, 2 * x + jnp.where(h == 0, c[0], 1 - c[0]))
    )
    return call(
        weight_grad_kernel,
        1,
        (2, 2),
        rows + [whole(d.shape) for d in deltas],
        [out] * len(deltas),
        [jax.ShapeDtypeStruct((units, 4 * width), BF)] * len(deltas),
        "weight_grads",
    )(core, mine, theirs, *deltas)


def spots(left, axis):
    strides = {name: RING ** (len(left) - 1 - i) for i, name in enumerate(left)}
    others = [name for name in left if name != axis]
    for number, places in enumerate(itertools.product(range(RING), repeat=len(others))):
        yield number, sum(p * strides[o] for p, o in zip(places, others)), strides[axis]


def along(place_ref, axis, shift):
    return lax.rem(place_ref[1 + AXES.index(axis)] + shift, RING)


def by_part(refs):
    return list(refs[:RING]), [refs[RING].at[i] for i in range(RING)]


def cut(left, part, stage, place_ref, load, pieces):
    axis = PARTS[part][2][stage]
    for i, piece in enumerate(pieces):
        there = along(place_ref, axis, SHIFTS[i]) if part == 0 else i
        for number, base, stride in spots(left, axis):
            load(base + stride * there, piece, number)


def sums_kernel(place_ref, mine, theirs, gate, up, down, their_gate, their_up, their_down, *refs):
    pieces, whole_ref = refs[:-1], refs[-1]
    x, n = pl.program_id(0), pl.program_id(1)
    units, step = gate.shape[1], 2
    outputs = (
        ((0, down, their_down),),
        ((1, gate, their_gate), (2, up, their_up)),
    )
    for first in range(0, gate.shape[0], step):
        at = slice(first * gate.shape[2], (first + step) * gate.shape[2])
        for t, terms in enumerate(outputs):
            total = None
            for i, own, other in terms:
                for rows, weight in ((mine, own), (theirs, other)):
                    part = jnp.dot(
                        rows[i, :, :units], wide(weight, first, step), preferred_element_type=F32
                    )
                    total = part if total is None else total + part
            rows_of = whole_ref.shape[3]
            total = total.reshape(-1, rows_of, total.shape[1]).astype(BF)
            whole_ref[t, n, pl.ds(x * total.shape[0], total.shape[0]), :, at] = total

    @pl.when((x == 1) & (n == 1))
    def _():
        half = whole_ref.shape[4]
        for p, (low, high, _) in enumerate(PARTS):

            def load(spot, piece, number):
                for t in range(2):
                    for m in range(2):
                        lo, hi = max(low, m * half), min(high, (m + 1) * half)
                        if lo < hi:
                            piece[t, number, :, lo - low : hi - low] = whole_ref[
                                t, m, spot, :, lo - m * half : hi - m * half
                            ]

            cut(AXES, p, 0, place_ref, load, by_part(pieces)[p])


def piece_shapes(rows):
    lead = (2, RING**2, rows)
    width = [high - low for low, high, _ in PARTS]
    first = jax.ShapeDtypeStruct(lead + (width[0],), BF)
    return [first] * RING + [jax.ShapeDtypeStruct((RING, *lead, width[1]), BF)]


def first_pieces(place, mine, theirs, cols, their_cols):
    _, tokens, padded = mine.shape
    blocks, units, depth = cols[0].shape
    per = blocks // 8
    rows = tokens // BLK
    shapes = piece_shapes(rows)
    return call(
        sums_kernel,
        1,
        (2, 2),
        [whole(mine.shape)] * 2
        + [pl.BlockSpec((per, units, depth), lambda x, n, c: (4 * x + 2 * c[0] + n, 0, 0))] * 3
        + [pl.BlockSpec((per, units, depth), lambda x, n, c: (2 * x + n, 0, 0))] * 3,
        [whole(shape.shape) for shape in shapes],
        shapes,
        "token_sums",
        scratch=[pltpu.VMEM((2, 2, 2 * BLK, rows, per * depth), BF)],
    )(place, mine, theirs, *cols, *their_cols)


def added(pieces):
    return sum(piece.astype(F32) for piece in pieces).astype(BF)


def add_first_kernel(place_ref, *refs):
    pieces, outs = by_part(refs[: RING + 1]), refs[RING + 1 :]

    def load(spot, piece, number):
        piece[0, number] = added([ref[0, spot] for ref in pieces[0]])

    left = [name for name in AXES if name != PARTS[0][2][0]]
    cut(left, 0, 1, place_ref, load, outs[:RING])
    for spot in range(RING**2):
        outs[RING][spot, 0] = added([ref[0, spot] for ref in pieces[1]])


def add_second_kernel(place_ref, *refs):
    pieces, outs = refs[:RING], refs[RING:]

    def load(spot, piece, number):
        piece[0] = added([ref[0, spot] for ref in pieces])

    cut([PARTS[0][2][2]], 0, 2, place_ref, load, outs)


def add_last_kernel(place_ref, *refs):
    pieces, second, outs = refs[:RING], refs[RING], refs[RING + 1 :]
    (low, middle, _), (_, high, _) = PARTS
    for t, out in enumerate(outs):
        out[:, low:middle] = added([ref[t] for ref in pieces])
        out[:, middle:high] = added([second[i, t] for i in range(second.shape[0])])


def each_result(kernel, place, arrays, shapes):
    def spec(shape, stacked):
        if stacked:
            return pl.BlockSpec(
                (shape[0], 1, *shape[2:]), lambda t, *_: (0, t) + (0,) * (len(shape) - 2)
            )
        return pl.BlockSpec((1, *shape[1:]), lambda t, *_: (t,) + (0,) * (len(shape) - 1))

    return call(
        kernel,
        1,
        (2,),
        [spec(array.shape, i >= RING) for i, array in enumerate(arrays)],
        [spec(shape.shape, i >= RING) for i, shape in enumerate(shapes)],
        shapes,
        "add_pieces",
    )(place, *arrays)


def axes_of(order):
    return sum(({"x": ("xh", "xl")}.get(name, (name,)) for name in order), ())


def to_shifts(stage, pieces):
    got = [pieces[0]]
    for piece, shift in zip(pieces[1:], SHIFTS[1:]):
        there = [(j, (j + shift) % RING) for j in range(RING)]
        got.append(lax.ppermute(piece, axes_of(PARTS[0][2][stage]), there))
    return got


def reduced(place, pieces):
    rows, width = pieces[0].shape[-2:]
    other = PARTS[1][1] - PARTS[1][0]
    one = jax.ShapeDtypeStruct((2, RING, rows, width), BF)
    many = jax.ShapeDtypeStruct((RING**2, 2, rows, other), BF)
    *first, second = each_result(add_first_kernel, place, pieces, [one] * RING + [many])
    left = "".join(name for name in AXES if name != PARTS[1][2][0])
    second = lax.all_to_all(second, axes_of(left), 0, 0, tiled=True)
    one = jax.ShapeDtypeStruct((2, rows, width), BF)
    first = each_result(add_second_kernel, place, to_shifts(1, first), [one] * RING)
    arrays = to_shifts(2, first) + [second]
    result = jax.ShapeDtypeStruct((rows, PARTS[1][1]), BF)
    return call(
        add_last_kernel,
        1,
        (1,),
        [whole(array.shape) for array in arrays],
        [whole(result.shape)] * 2,
        [result] * 2,
        "add_last",
    )(place, *arrays)


def over_core(x):
    return lax.ppermute(x, "c", [(0, 1), (1, 0)])


def half_blocks(cols, half):
    blocks, units, depth = cols.shape
    cut = cols.reshape(2, 2, blocks // 4, units, depth)
    picked = lax.dynamic_index_in_dim(cut, half, 1, keepdims=False)
    return picked.reshape(blocks // 2, units, depth)


def route_columns(ids, gates):
    columns, rest = [ids.astype(F32)], gates
    for _ in range(3):
        piece = lax.reduce_precision(rest, 8, 7)
        columns.append(piece)
        rest = rest - piece
    columns = jnp.concatenate(columns, axis=1)
    return jnp.pad(columns, ((0, 0), (0, 128 - columns.shape[1]))).astype(BF)


def routes(columns):
    columns = columns.reshape(-1, columns.shape[-1])[:, :8].astype(F32)
    gates = columns[:, 2:4] + columns[:, 4:6] + columns[:, 6:8]
    return columns[:, :2].astype(jnp.int32), gates


def slot_tables(ids, gates, expert):
    matched = ids == expert
    chosen = jnp.any(matched, axis=-1)
    gate = jnp.sum(jnp.where(matched, gates, F32(0.0)), axis=-1)
    counted = chosen.reshape(BLK, -1).astype(jnp.int32)
    position = jnp.cumsum(counted, axis=1) - counted
    per_group = BLK // GROUPS
    slots = per_group * CAP
    base = (lax.broadcasted_iota(jnp.int32, position.shape, 0) % per_group) * CAP
    slot = jnp.where(counted == 1, base + position, -1).reshape(GROUPS, -1)
    shape = (GROUPS, slots, slot.shape[1])
    selector = lax.broadcasted_iota(jnp.int32, shape, 1) == slot[:, None, :]
    slot_gate = jnp.sum(jnp.where(selector, gate.reshape(GROUPS, 1, -1), F32(0.0)), axis=2)
    spread = lax.broadcasted_iota(jnp.int32, (GROUPS, slot.shape[1], slots), 2) == slot[:, :, None]
    return selector.astype(BF), spread.astype(BF), slot_gate.reshape(-1, 1)


def average(attention):
    me = lax.axis_index(BRANCH)
    share = attention.shape[1] // 4

    def quarter(i):
        return lax.dynamic_slice_in_dim(attention, i * share, share, 1)

    total = quarter(me).astype(F32)
    for shift in range(1, 4):
        sent = quarter((me + shift) % 4)
        there = [(i, (i + shift) % 4) for i in range(4)]
        total = total + lax.ppermute(sent, BRANCH, there).astype(F32)
    return (total / 4).astype(BF)


def together(*arrays):
    return lax.optimization_barrier(arrays)


def on_device(
    attention_out, tokens, out_grads, route_ids, route_gates, gate_weight, up_weight, down_weight
):
    core = lax.axis_index("c")
    expert_id = 2 * lax.axis_index("xh") + core
    sibling = 2 * lax.axis_index("xh") + 1 - core
    core_id = core.reshape(1).astype(jnp.int32)

    width = tokens.shape[1]
    both = jnp.concatenate([tokens, out_grads, route_columns(route_ids, route_gates)], axis=1)
    gathered = lax.all_gather(both, PLANE, axis=0, tiled=True)
    gathered = gathered.reshape(2, GROUPS, -1, both.shape[1])

    gate_blocks = transposed(gate_weight)
    up_blocks, down_blocks = transposed(up_weight), transposed(down_weight)
    gate_cols = to_owners(gate_blocks)
    merged_attention = average(attention_out[0])
    gate_cols, up_blocks, down_blocks, merged_attention = together(
        gate_cols, up_blocks, down_blocks, merged_attention
    )
    their_gate = over_core(half_blocks(gate_cols, 1 - core))
    up_cols = to_owners(up_blocks)
    up_cols, down_blocks = together(up_cols, down_blocks)
    their_up = over_core(half_blocks(up_cols, 1 - core))
    down_cols = to_owners(down_blocks)
    down_cols, gathered, their_gate, their_up = together(
        down_cols, gathered, their_gate, their_up
    )

    ids, gates = routes(gathered[0, :, :, 2 * width :])
    selector, spread, slot_gate = slot_tables(ids, gates, expert_id)
    other_selector, _, other_gate = slot_tables(ids, gates, sibling)
    theirs = over_core(picked_rows(other_selector, other_gate, gathered))
    their_down = over_core(half_blocks(down_cols, 1 - core))
    mine = picked_rows(selector, slot_gate, gathered)
    mine, theirs, their_down = together(mine, theirs, their_down)
    hidden, gate_delta, up_delta, by_token = expert(
        core_id, mine, theirs, gate_cols, up_cols, down_cols, slot_gate, spread
    )
    their_token = over_core(by_token)
    place = jnp.stack(
        [core, 2 * lax.axis_index("xh") + lax.axis_index("xl"), lax.axis_index("z"), lax.axis_index("y")]
    ).astype(jnp.int32)
    pieces = first_pieces(
        place,
        by_token,
        their_token,
        (gate_cols, up_cols, down_cols),
        (their_gate, their_up, their_down),
    )
    got = to_shifts(0, pieces[:RING])
    got.append(lax.all_to_all(pieces[RING], axes_of(PARTS[1][2][0]), 0, 0, tiled=True))
    gate_grads, up_grads = weight_grads(core_id, mine, theirs, 0, [gate_delta, up_delta])
    (down_grads,) = weight_grads(core_id, mine, theirs, 1, [hidden])
    *got, gate_grads, up_grads, down_grads = together(*got, gate_grads, up_grads, down_grads)
    mixed_out, token_grads = reduced(place, got)
    return (
        merged_attention,
        mixed_out,
        token_grads,
        gate_grads.T[None],
        up_grads.T[None],
        down_grads.T[None],
    )


def solution(mesh):
    fine = Mesh(mesh.devices.reshape(2, 2, 2, 4, 4), ("xh", "c", "xl", "z", "y"))
    return jax.shard_map(
        on_device,
        mesh=fine,
        in_specs=(
            P(BRANCH, FSDP, None),
            P(FSDP, BRANCH),
            P(FSDP, BRANCH),
            P(FSDP, None),
            P(FSDP, None),
            P(BRANCH, FSDP, None),
            P(BRANCH, FSDP, None),
            P(BRANCH, FSDP, None),
        ),
        out_specs=(
            P(FSDP, BRANCH),
            P(FSDP, BRANCH),
            P(FSDP, BRANCH),
            P(BRANCH, None, FSDP),
            P(BRANCH, None, FSDP),
            P(BRANCH, None, FSDP),
        ),
        check_vma=False,
    )
```
